512 devices in a mesh: seq: 32 (over x, y), head: 16 (over z, core).
Axes of the slice: x: 4, y: 8, z: 8, core: 2. Of those that a mesh axis runs over, the one named last changes fastest.
Arguments:
- queries: bfloat16 [32768, 6144], P('seq', 'head'), may hold values from -64 to 64
- text: bfloat16 [512, 6144], P(None, 'seq'), may hold values from -6 to 6
- key_weight: bfloat16 [6144, 6144], P('seq', 'head'), may hold values from -0.078125 to 0.078125
- value_weight: bfloat16 [6144, 6144], P('seq', 'head'), may hold values from -0.078125 to 0.078125
- out_grad: bfloat16 [32768, 6144], P('seq', 'head'), may hold values from -6 to 6
Outputs:
- attn_out: bfloat16 [32768, 6144], P('seq', 'head')
- query_grad: bfloat16 [32768, 6144], P('seq', 'head')
- key_weight_grad: float32 [6144, 6144], P('seq', 'head')
- value_weight_grad: float32 [6144, 6144], P('seq', 'head')
- text_grad: float32 [512, 6144], P('head', 'seq')
The draws below stay inside these ranges and needn't reach their ends.
All inputs are finite; a program needn't handle non-finite values.
Results may differ from the reference program's by a relative error of at most 0.006.
The reference program's roundings to bfloat16 on the way (of `probs_low` and `dscores`) count: a program that leaves them out, or rounds other values in their place, can miss the bound.
Values may be sent and summed in bfloat16 or wider, within the bound.
A program may use at most 64 MiB of HBM per device.

```python
import jax
import jax.numpy as jnp
from jax import lax

D = 6144
HEADS = 48
HS = 128
TEXT = 512
QROWS = 32768


def draw_queries(key, part):
    first = jax.random.fold_in(jax.random.fold_in(key, 7), 0)
    values = jnp.clip(jax.random.normal(first, (QROWS, HEADS * HS), jnp.float32), -6.0, 6.0)
    return values.astype(jnp.bfloat16)


def steps_of(own_key, dims, pieces, low, high):
    level, own = 1.0, jax.random.fold_in(own_key, 6)
    for dim, shards_of in pieces:
        draws = jnp.exp(jax.random.uniform(jax.random.fold_in(own, dim), (shards_of,), jnp.float32, low / len(pieces), high / len(pieces)))
        level = level * jnp.repeat(draws, dims[dim] // shards_of).reshape([-1 if axis == dim else 1 for axis in range(len(dims))])
    return level


def scatter_about(rng, dims, width, most, cuts=(), kind=jnp.bfloat16):
    factor_of = steps_of(rng, dims, cuts, -0.22, 0.18) if cuts else 1.0
    result = jax.random.normal(rng, dims, jnp.float32) * width * factor_of
    return jnp.minimum(jnp.maximum(result, -most), most).astype(kind)


def setup_inputs(seed: int = 0) -> dict:
    splits = jax.random.split(jax.random.key(seed), 6)
    queries = draw_queries(jax.random.fold_in(splits[5], 71), 0)
    text = scatter_about(splits[1], (TEXT, D), 1.0, 6.0, ((1, 32),))
    key_weight = scatter_about(splits[2], (D, HEADS * HS), D ** -0.5, 0.078125, ((0, 32), (1, 16)))
    value_weight = scatter_about(splits[3], (D, HEADS * HS), D ** -0.5, 0.078125, ((0, 32), (1, 16)))
    out_grad = scatter_about(splits[4], (QROWS, HEADS * HS), 1.0, 6.0, ((0, 32), (1, 16)))
    return dict(queries=queries, text=text, key_weight=key_weight, value_weight=value_weight, out_grad=out_grad)


def per_head(items):
    query_head, grad_head, key_head, value_head = items
    score_scale = 1.0 / (HS ** 0.5)
    scores = jnp.dot(query_head, key_head.T, preferred_element_type=jnp.float32) * score_scale
    probs = jax.nn.softmax(scores, axis=-1)
    probs_low = probs.astype(jnp.bfloat16)
    output = jnp.dot(probs_low, value_head, preferred_element_type=jnp.float32).astype(jnp.bfloat16)
    dprobs = jnp.dot(grad_head, value_head.T, preferred_element_type=jnp.float32)
    delta = jnp.sum(probs * dprobs, axis=-1, keepdims=True)
    dscores = (probs * (dprobs - delta) * score_scale).astype(jnp.bfloat16)
    query_part = jnp.dot(dscores, key_head, preferred_element_type=jnp.float32).astype(jnp.bfloat16)
    key_part = jnp.dot(dscores.T, query_head, preferred_element_type=jnp.float32)
    value_part = jnp.dot(probs_low.T, grad_head, preferred_element_type=jnp.float32)
    return output, query_part, key_part, value_part


def split_heads(matrix, count):
    return matrix.reshape(count, HEADS, HS).transpose(1, 0, 2)


def join_heads(stacked, count):
    return stacked.transpose(1, 0, 2).reshape(count, HEADS * HS)


def reference(queries, text, key_weight, value_weight, out_grad):
    key_rows = jnp.dot(text, key_weight, preferred_element_type=jnp.float32).astype(jnp.bfloat16)
    value_rows = jnp.dot(text, value_weight, preferred_element_type=jnp.float32).astype(jnp.bfloat16)
    results = lax.map(per_head, (split_heads(queries, QROWS), split_heads(out_grad, QROWS),
                                 split_heads(key_rows, TEXT), split_heads(value_rows, TEXT)))
    attn_out = join_heads(results[0], QROWS)
    query_grad = join_heads(results[1], QROWS)
    key_grad = join_heads(results[2], TEXT).astype(jnp.bfloat16)
    value_grad = join_heads(results[3], TEXT).astype(jnp.bfloat16)
    key_weight_grad = jnp.dot(text.T, key_grad, preferred_element_type=jnp.float32)
    value_weight_grad = jnp.dot(text.T, value_grad, preferred_element_type=jnp.float32)
    text_grad = (jnp.dot(key_grad, key_weight.T, preferred_element_type=jnp.float32)
                 + jnp.dot(value_grad, value_weight.T, preferred_element_type=jnp.float32))
    return attn_out, query_grad, key_weight_grad, value_weight_grad, text_grad
```

```python
import jax
import jax.numpy as jnp
from jax import lax
from jax.experimental import pallas as pl
from jax.experimental.pallas import tpu as pltpu
from jax.sharding import PartitionSpec as P

MESH = pl.DeviceIdType.MESH
NX, NY, NZ, NC = 4, 8, 8, 2
HS = 128
HEADS = 3
TEXT = 512
FEAT = 192
ROWS = 1024
XT = TEXT // NX
YT = XT // NY
ZT = TEXT // (NZ * NC)
RB = 256
NB = ROWS // RB
SCALE = 1.0 / HS**0.5
EXP2_SCALE = SCALE * 1.4426950408889634
BF = jnp.bfloat16
F32 = jnp.float32

S_KX, S_VX, S_KY, S_VY, S_AY, S_AX, S_GX, S_GY, S_GAY, S_GAX = range(10)


def dot(a, b):
    return jnp.dot(a, b, preferred_element_type=F32)


def kernel(
    q_hbm, tt_hbm, kw_hbm, vw_hbm, og_hbm,
    o_hbm, dq_hbm, kwg_hbm, vwg_hbm, tg_hbm,
    q_v, og_v, text_v, kw_v, vw_v, w_v,
    qt_v, ogt_v, tt_v, kt_v, vt_v,
    kp, vp, kx, vx, ks, vs, ky, vy, kvf,
    dk_acc, dv_acc, gp, gx, gs, gy, gf,
    o_v, dq_v, kwg_v, vwg_v, tp, tc, ts, tz, tg_v,
    in_sem, out_sem, ssem, rsem, fs_sem, fr_sem,
):
    seq = lax.axis_index("seq")
    head = lax.axis_index("head")
    mx, my = seq // NY, lax.rem(seq, NY)
    mz, mc = head // NC, lax.rem(head, NC)

    def x_peer(i):
        px = lax.rem(mx + i, NX)
        return px, (px * NY + my, head)

    def y_peer(i):
        py = lax.rem(my + i, NY)
        return py, (mx * NY + py, head)

    def z_peer(i):
        pz = lax.rem(mz + i, NZ)
        return pz, (seq, pz * NC + mc)

    core_peer = (seq, mz * NC + (1 - mc))

    barrier = pltpu.get_barrier_semaphore()
    peers = [x_peer(i)[1] for i in range(1, NX)] + [y_peer(i)[1] for i in range(1, NY)]
    peers += [z_peer(i)[1] for i in range(1, NZ)] + [core_peer]
    for peer in peers:
        pl.semaphore_signal(barrier, inc=1, device_id=peer, device_id_type=MESH)

    loads = [
        pltpu.make_async_copy(a, b, in_sem.at[i])
        for i, (a, b) in enumerate(
            ((tt_hbm, tt_v), (kw_hbm, kw_v), (vw_hbm, vw_v), (q_hbm, q_v), (og_hbm, og_v))
        )
    ]
    for load in loads:
        load.start()

    def send(src, dst, h, stage, device):
        pltpu.make_async_remote_copy(
            src_ref=src, dst_ref=dst, send_sem=ssem.at[h, stage], recv_sem=rsem.at[h, stage],
            device_id=device, device_id_type=MESH,
        ).start()

    def bytes_of(h, stage):
        return {
            S_KX: kx.at[h, pl.ds(0, NX - 1)],
            S_VX: vx.at[h, pl.ds(0, NX - 1)],
            S_KY: ky.at[h, pl.ds(0, NY - 1)],
            S_VY: vy.at[h, pl.ds(0, NY - 1)],
            S_AY: kvf.at[h, 0, pl.ds(0, NY - 1)],
            S_AX: kvf.at[h, pl.ds(0, NX - 1)],
            S_GX: gx.at[h, pl.ds(0, NX - 1)],
            S_GY: gy.at[h, pl.ds(0, NY - 1)],
            S_GAY: gf.at[h, 0, pl.ds(0, NY - 1)],
            S_GAX: gf.at[h, pl.ds(0, NX - 1)],
        }[stage]

    def wait(sem, h, stage):
        ref = bytes_of(h, stage)
        pltpu.make_async_copy(ref, ref, sem.at[h, stage]).wait()

    def project(h):
        cols = slice(h * HS, (h + 1) * HS)
        kp[h] = dot(text_v[...], kw_v[:, cols]).reshape(NX, NY, YT, HS)
        vp[h] = dot(text_v[...], vw_v[:, cols]).astype(BF).reshape(NX, NY, YT, HS)

    def f_x(h):
        for i in (2, 1, 3):
            px, device = x_peer(i)
            send(kp.at[h, px], kx.at[h, mx], h, S_KX, device)
            send(vp.at[h, px], vx.at[h, mx], h, S_VX, device)

    def f_y(h):
        wait(rsem, h, S_KX)
        wait(rsem, h, S_VX)
        k = kp[h, mx]
        v = vp[h, mx].astype(F32)
        for i in range(1, NX):
            k = k + kx[h, x_peer(i)[0]]
            v = v + vx[h, x_peer(i)[0]].astype(F32)
        ks[h] = k
        vs[h] = v.astype(BF)
        for i in (4, 3, 5, 2, 6, 1, 7):
            py, device = y_peer(i)
            send(ks.at[h, py], ky.at[h, my], h, S_KY, device)
            send(vs.at[h, py], vy.at[h, my], h, S_VY, device)

    def f_ay(h):
        wait(rsem, h, S_KY)
        wait(rsem, h, S_VY)
        k = ks[h, my]
        v = vs[h, my].astype(F32)
        for i in range(1, NY):
            k = k + ky[h, y_peer(i)[0]]
            v = v + vy[h, y_peer(i)[0]].astype(F32)
        kvf[h, mx, my, :, :HS] = k.astype(BF)
        kvf[h, mx, my, :, HS:] = v.astype(BF)
        for i in (4, 3, 5, 2, 6, 1, 7):
            send(kvf.at[h, mx, my], kvf.at[h, mx, my], h, S_AY, y_peer(i)[1])

    def f_ax(h):
        wait(rsem, h, S_AY)
        for i in (2, 1, 3):
            send(kvf.at[h, mx], kvf.at[h, mx], h, S_AX, x_peer(i)[1])

    def attend(h):
        wait(rsem, h, S_AX)
        cols = slice(h * HS, (h + 1) * HS)
        kt_v[...] = kvf[h, :, :, :, :HS].reshape(TEXT, HS).T
        vt_v[...] = kvf[h, :, :, :, HS:].reshape(TEXT, HS).T
        dk_acc[...] = jnp.zeros_like(dk_acc)
        dv_acc[...] = jnp.zeros_like(dv_acc)

        def block(b, carry):
            rows = pl.ds(pl.multiple_of(b * RB, RB), RB)
            k = kvf[h, :, :, :, :HS].reshape(TEXT, HS)
            v = kvf[h, :, :, :, HS:].reshape(TEXT, HS)
            s = dot(k, qt_v[h, b])
            e = jnp.exp2((s - jnp.max(s, axis=0, keepdims=True)) * EXP2_SCALE)
            p = e * (1.0 / jnp.sum(e, axis=0, keepdims=True))
            low = p.astype(BF)
            o_v[h, rows, :] = dot(vt_v[...], low).T.astype(BF)
            dp = dot(v, ogt_v[h, b])
            delta = jnp.sum(p * dp, axis=0, keepdims=True)
            ds = (p * (dp - delta) * SCALE).astype(BF)
            dq_v[h, rows, :] = dot(kt_v[...], ds).T.astype(BF)
            dk_acc[...] += dot(ds, q_v[rows, cols])
            dv_acc[...] += dot(low, og_v[rows, cols])
            return carry

        lax.fori_loop(0, NB, block, 0)
        for i, (a, b) in enumerate(((o_v, o_hbm), (dq_v, dq_hbm))):
            pltpu.make_async_copy(a.at[h], b.at[:, pl.ds(h * HS, HS)], out_sem.at[h, i]).start()
        gp[h, :, :, :, :HS] = dk_acc[...].astype(BF).reshape(NX, NY, YT, HS)
        gp[h, :, :, :, HS:] = dv_acc[...].astype(BF).reshape(NX, NY, YT, HS)
        for i in (2, 1, 3):
            px, device = x_peer(i)
            send(gp.at[h, px], gx.at[h, mx], h, S_GX, device)

    def b_y(h):
        wait(rsem, h, S_GX)
        g = gp[h, mx].astype(F32)
        for i in range(1, NX):
            g = g + gx[h, x_peer(i)[0]].astype(F32)
        gs[h] = g.astype(BF)
        for i in (4, 3, 5, 2, 6, 1, 7):
            py, device = y_peer(i)
            send(gs.at[h, py], gy.at[h, my], h, S_GY, device)

    def b_ay(h):
        wait(rsem, h, S_GY)
        g = gs[h, my].astype(F32)
        for i in range(1, NY):
            g = g + gy[h, y_peer(i)[0]].astype(F32)
        gf[h, mx, my] = g.astype(BF)
        for i in (4, 3, 5, 2, 6, 1, 7):
            send(gf.at[h, mx, my], gf.at[h, mx, my], h, S_GAY, y_peer(i)[1])

    def b_ax(h):
        wait(rsem, h, S_GAY)
        for i in (2, 1, 3):
            send(gf.at[h, mx], gf.at[h, mx], h, S_GAX, x_peer(i)[1])

    def finish(h):
        wait(rsem, h, S_GAX)
        cols = slice(h * HS, (h + 1) * HS)
        g = gf[h].reshape(TEXT, 2 * HS)
        part = lax.dot_general(g, w_v[h], (((1,), (1,)), ((), ())), preferred_element_type=F32)
        part = part.reshape(NZ, NC, ZT, FEAT)
        if h == 0:
            tp[...] = part
        else:
            tp[...] += part
        if h == HEADS - 1:
            pltpu.make_async_remote_copy(
                src_ref=tp.at[:, 1 - mc], dst_ref=tc, send_sem=fs_sem.at[0], recv_sem=fr_sem.at[0],
                device_id=core_peer, device_id_type=MESH,
            ).start()
        wg = dot(tt_v[...], g)
        kwg_v[:, cols] = wg[:, :HS]
        vwg_v[:, cols] = wg[:, HS:]

    for i in range(3):
        loads[i].wait()
    text_v[...] = tt_v[...].T
    for h in range(HEADS):
        project(h)
        if h == 0:
            pl.semaphore_wait(barrier, len(peers))
        f_x(h)
    for i in range(3, 5):
        loads[i].wait()
    for h in range(HEADS):
        cols = slice(h * HS, (h + 1) * HS)
        w_v[h, :, :HS] = kw_v[:, cols]
        w_v[h, :, HS:] = vw_v[:, cols]

        def turn(b, carry, h=h, cols=cols):
            rows = pl.ds(pl.multiple_of(b * RB, RB), RB)
            qt_v[h, b] = q_v[rows, cols].T
            ogt_v[h, b] = og_v[rows, cols].T
            return carry

        lax.fori_loop(0, NB, turn, 0)
    f_y(0)
    f_y(1)
    f_ay(0)
    f_y(2)
    f_ay(1)
    f_ax(0)
    f_ay(2)
    f_ax(1)
    f_ax(2)
    attend(0)
    attend(1)
    b_y(0)
    attend(2)
    b_ay(0)
    b_y(1)
    b_ax(0)
    b_ay(1)
    b_y(2)
    b_ax(1)
    b_ay(2)
    finish(0)
    b_ax(2)
    finish(1)
    finish(2)

    pltpu.make_async_copy(kwg_v, kwg_hbm, out_sem.at[HEADS, 0]).start()
    pltpu.make_async_copy(vwg_v, vwg_hbm, out_sem.at[HEADS, 1]).start()

    def final_wait(sem, i, ref):
        pltpu.make_async_copy(ref, ref, sem.at[i]).wait()

    final_wait(fr_sem, 0, tc)
    ts[...] = (tp[:, mc] + tc[...]).astype(BF)
    for i in (4, 3, 5, 2, 6, 1, 7):
        pz, device = z_peer(i)
        pltpu.make_async_remote_copy(
            src_ref=ts.at[pz], dst_ref=tz.at[mz], send_sem=fs_sem.at[1], recv_sem=fr_sem.at[1],
            device_id=device, device_id_type=MESH,
        ).start()
    for h in range(HEADS):
        for stage in range(10):
            wait(ssem, h, stage)
        for i, (a, b) in enumerate(((o_v, o_hbm), (dq_v, dq_hbm))):
            pltpu.make_async_copy(a.at[h], b.at[:, pl.ds(h * HS, HS)], out_sem.at[h, i]).wait()
    final_wait(fs_sem, 0, tc)
    final_wait(fr_sem, 1, tz.at[pl.ds(0, NZ - 1)])
    t = tp[mz, mc] + tc[mz]
    for i in range(1, NZ):
        t = t + tz[z_peer(i)[0]].astype(F32)
    tg_v[...] = t
    last = pltpu.make_async_copy(tg_v, tg_hbm, out_sem.at[HEADS, 2])
    last.start()
    pltpu.make_async_copy(kwg_v, kwg_hbm, out_sem.at[HEADS, 0]).wait()
    pltpu.make_async_copy(vwg_v, vwg_hbm, out_sem.at[HEADS, 1]).wait()
    final_wait(fs_sem, 1, tz.at[pl.ds(0, NZ - 1)])
    last.wait()


def local(queries, text, key_weight, value_weight, out_grad):
    width = HEADS * HS
    vm = pltpu.VMEM
    dma = pltpu.SemaphoreType.DMA
    return pl.pallas_call(
        kernel,
        name="cross_attention",
        out_shape=(
            jax.ShapeDtypeStruct((ROWS, width), BF),
            jax.ShapeDtypeStruct((ROWS, width), BF),
            jax.ShapeDtypeStruct((FEAT, width), F32),
            jax.ShapeDtypeStruct((FEAT, width), F32),
            jax.ShapeDtypeStruct((ZT, FEAT), F32),
        ),
        in_specs=[pl.BlockSpec(memory_space=pl.ANY)] * 5,
        out_specs=tuple([pl.BlockSpec(memory_space=pl.ANY)] * 5),
        scratch_shapes=[
            vm((ROWS, width), BF), vm((ROWS, width), BF), vm((TEXT, FEAT), BF),
            vm((FEAT, width), BF), vm((FEAT, width), BF), vm((HEADS, FEAT, 2 * HS), BF),
            vm((HEADS, NB, HS, RB), BF), vm((HEADS, NB, HS, RB), BF), vm((FEAT, TEXT), BF),
            vm((HS, TEXT), BF), vm((HS, TEXT), BF),
            vm((HEADS, NX, NY, YT, HS), F32), vm((HEADS, NX, NY, YT, HS), BF),
            vm((HEADS, NX, NY, YT, HS), F32), vm((HEADS, NX, NY, YT, HS), BF),
            vm((HEADS, NY, YT, HS), F32), vm((HEADS, NY, YT, HS), BF),
            vm((HEADS, NY, YT, HS), F32), vm((HEADS, NY, YT, HS), BF),
            vm((HEADS, NX, NY, YT, 2 * HS), BF),
            vm((TEXT, HS), F32), vm((TEXT, HS), F32),
            vm((HEADS, NX, NY, YT, 2 * HS), BF), vm((HEADS, NX, NY, YT, 2 * HS), BF),
            vm((HEADS, NY, YT, 2 * HS), BF), vm((HEADS, NY, YT, 2 * HS), BF),
            vm((HEADS, NX, NY, YT, 2 * HS), BF),
            vm((HEADS, ROWS, HS), BF), vm((HEADS, ROWS, HS), BF),
            vm((FEAT, width), F32), vm((FEAT, width), F32),
            vm((NZ, NC, ZT, FEAT), F32), vm((NZ, ZT, FEAT), F32),
            vm((NZ, ZT, FEAT), BF), vm((NZ, ZT, FEAT), BF), vm((ZT, FEAT), F32),
            dma((5,)), dma((HEADS + 1, 3)), dma((HEADS, 10)), dma((HEADS, 10)), dma((2,)), dma((2,)),
        ],
        compiler_params=pltpu.CompilerParams(
            collective_id=0, has_side_effects=True, vmem_limit_bytes=56 * 1024 * 1024
        ),
    )(queries, text.T, key_weight, value_weight, out_grad)


def solution(mesh):
    in_specs = (
        P("seq", "head"),
        P(None, "seq"),
        P("seq", "head"),
        P("seq", "head"),
        P("seq", "head"),
    )
    out_specs = (
        P("seq", "head"),
        P("seq", "head"),
        P("seq", "head"),
        P("seq", "head"),
        P("head", "seq"),
    )
    return jax.shard_map(local, mesh=mesh, in_specs=in_specs, out_specs=out_specs, check_vma=False)
```

```python
import jax
import jax.numpy as jnp
from jax import lax
from jax.experimental import pallas as pl
from jax.experimental.pallas import tpu as pltpu
from jax.sharding import PartitionSpec as P

MESH = pl.DeviceIdType.MESH
NX, NY, NZ, NC = 4, 8, 8, 2
HS = 128
HEADS = 3
TEXT = 512
FEAT = 192
ROWS = 1024
TH = TEXT // 2
YT = TH // NY
FH = FEAT // 2
ZT = TEXT // (NZ * NC)
SCALE = 1.0 / HS**0.5
EXP2_SCALE = SCALE * 1.4426950408889634
BF = jnp.bfloat16
F32 = jnp.float32

S_W, S_Y, S_AY, S_AX, S_GX, S_GY, S_GAY, S_GAX = range(8)
FAR_FIRST = (4, 3, 5, 2, 6, 1, 7)


def dot(a, b):
    return jnp.dot(a, b, preferred_element_type=F32)


def kernel(
    q_hbm, tt_hbm, kw_hbm, vw_hbm, og_hbm,
    o_ref, dq_ref, kwg_ref, vwg_ref, tg_ref,
    q_v, og_v, tt_v, w_v, tx, wx, txt, qt_v, ogt_v,
    ks, ky, kvf, gp, gx, gs, gy, gf,
    tp, tc, ts, tz,
    in_sem, ssem, rsem, fs_sem, fr_sem,
):
    seq = lax.axis_index("seq")
    head = lax.axis_index("head")
    mx, my = seq // NY, lax.rem(seq, NY)
    mz, mc = head // NC, lax.rem(head, NC)
    mb, ma = mx // 2, lax.rem(mx, 2)

    def x_peer(i):
        px = lax.rem(mx + i, NX)
        return px, (px * NY + my, head)

    def y_peer(i):
        py = lax.rem(my + i, NY)
        return py, (mx * NY + py, head)

    def z_peer(i):
        pz = lax.rem(mz + i, NZ)
        return pz, (seq, pz * NC + mc)

    core_peer = (seq, mz * NC + (1 - mc))

    barrier = pltpu.get_barrier_semaphore()
    peers = [x_peer(i)[1] for i in range(1, NX)] + [y_peer(i)[1] for i in range(1, NY)]
    peers += [z_peer(i)[1] for i in range(1, NZ)] + [core_peer]
    for peer in peers:
        pl.semaphore_signal(barrier, inc=1, device_id=peer, device_id_type=MESH)

    loads = []
    for a in range(2):
        for c in range(NC):
            loads.append((tt_hbm.at[pl.ds(c * FH, FH), pl.ds(a * TH, TH)], tt_v.at[a, c]))
    for h in range(HEADS):
        loads.append((kw_hbm.at[:, pl.ds(h * HS, HS)], w_v.at[0, h]))
        loads.append((vw_hbm.at[:, pl.ds(h * HS, HS)], w_v.at[1, h]))
    loads += [(q_hbm, q_v), (og_hbm, og_v)]
    loads = [pltpu.make_async_copy(a, b, in_sem.at[i]) for i, (a, b) in enumerate(loads)]
    for load in loads:
        load.start()

    def copy_to(src, dst, s_sem, r_sem, device):
        pltpu.make_async_remote_copy(
            src_ref=src, dst_ref=dst, send_sem=s_sem, recv_sem=r_sem,
            device_id=device, device_id_type=MESH,
        ).start()

    def send(src, dst, h, stage, device):
        copy_to(src, dst, ssem.at[h, stage], rsem.at[h, stage], device)

    def wait_bytes(sem, ref):
        pltpu.make_async_copy(ref, ref, sem).wait()

    def wait(sem, h, stage):
        ref = {
            S_W: wx.at[h, pl.ds(0, NX - 1)],
            S_Y: ky.at[h, pl.ds(0, NY - 1)],
            S_AY: kvf.at[h, 0, pl.ds(0, NY - 1)],
            S_AX: kvf.at[h, pl.ds(0, NX - 1)],
            S_GX: gx.at[h, pl.ds(0, NX - 1)],
            S_GY: gy.at[h, pl.ds(0, NY - 1)],
            S_GAY: gf.at[h, 0, pl.ds(0, NY - 1)],
            S_GAX: gf.at[h, pl.ds(0, NX - 1)],
        }[stage]
        wait_bytes(sem.at[h, stage], ref)

    def spread_y(full, h, stage):
        for i in FAR_FIRST:
            send(full.at[h, mx, my], full.at[h, mx, my], h, stage, y_peer(i)[1])

    def spread_x(full, h, before, stage):
        wait(rsem, h, before)
        for i in (2, 1, 3):
            send(full.at[h, mx], full.at[h, mx], h, stage, x_peer(i)[1])

    def f_w(h):
        for i in (2, 1, 3):
            px, device = x_peer(i)
            send(w_v.at[px // 2, h], wx.at[h, mx], h, S_W, device)

    def f_y(h):
        wait(rsem, h, S_W)
        p = dot(txt[mx], w_v[mb, h])
        for i in range(1, NX):
            px = x_peer(i)[0]
            p = p + dot(txt[px], wx[h, px])
        ks[h] = p.reshape(NY, YT, HS)
        for i in FAR_FIRST:
            py, device = y_peer(i)
            send(ks.at[h, py], ky.at[h, my], h, S_Y, device)

    def f_ay(h):
        wait(rsem, h, S_Y)
        k = ks[h, my]
        for i in range(1, NY):
            k = k + ky[h, y_peer(i)[0]]
        kvf[h, mx, my] = k.astype(BF)
        spread_y(kvf, h, S_AY)

    def f_ax(h):
        spread_x(kvf, h, S_AY, S_AX)

    def attend(h):
        wait(rsem, h, S_AX)
        cols = slice(h * HS, (h + 1) * HS)
        k = kvf[h, 0:2].reshape(TEXT, HS)
        v = kvf[h, 2:4].reshape(TEXT, HS)
        s = dot(k, qt_v[h])
        e = jnp.exp2((s - jnp.max(s, axis=0, keepdims=True)) * EXP2_SCALE)
        p = e * (1.0 / jnp.sum(e, axis=0, keepdims=True))
        low = p.astype(BF)
        dp = dot(v, ogt_v[h])
        delta = jnp.sum(p * dp, axis=0, keepdims=True)
        ds = (p * (dp - delta) * SCALE).astype(BF)
        gp[h, 2:4] = dot(low, og_v[:, cols]).astype(BF).reshape(2, NY, YT, HS)
        gp[h, 0:2] = dot(ds, q_v[:, cols]).astype(BF).reshape(2, NY, YT, HS)
        for i in (2, 1, 3):
            px, device = x_peer(i)
            send(gp.at[h, px], gx.at[h, mx], h, S_GX, device)
        o_ref[:, cols] = dot(v.T, low).T.astype(BF)
        dq_ref[:, cols] = dot(k.T, ds).T.astype(BF)

    def b_y(h):
        wait(rsem, h, S_GX)
        g = gp[h, mx].astype(F32)
        for i in range(1, NX):
            g = g + gx[h, x_peer(i)[0]].astype(F32)
        gs[h] = g.astype(BF)
        for i in FAR_FIRST:
            py, device = y_peer(i)
            send(gs.at[h, py], gy.at[h, my], h, S_GY, device)

    def b_ay(h):
        wait(rsem, h, S_GY)
        g = gs[h, my].astype(F32)
        for i in range(1, NY):
            g = g + gy[h, y_peer(i)[0]].astype(F32)
        gf[h, mx, my] = g.astype(BF)
        spread_y(gf, h, S_GAY)

    def b_ax(h):
        spread_x(gf, h, S_GAY, S_GAX)

    def finish(h):
        wait(rsem, h, S_GAX)
        cols = slice(h * HS, (h + 1) * HS)
        part = 0.0
        for j in range(2):
            g = gf[h, 2 * j : 2 * j + 2].reshape(TEXT, HS)
            part = part + lax.dot_general(
                g, w_v[j, h], (((1,), (1,)), ((), ())), preferred_element_type=F32
            )
        part = part.reshape(NZ, NC, ZT, FEAT)
        if h == 0:
            tp[...] = part
        else:
            tp[...] += part
        if h == HEADS - 1:
            copy_to(tp.at[:, 1 - mc], tc, fs_sem.at[0], fr_sem.at[0], core_peer)
        for j, ref in enumerate((kwg_ref, vwg_ref)):
            wg = 0.0
            for a in range(2):
                wg = wg + dot(tt_v[a].reshape(FEAT, TH), gf[h, 2 * j + a].reshape(TH, HS))
            ref[:, cols] = wg

    for load in loads:
        load.wait()
    txt[mx] = tt_v[ma].reshape(FEAT, TH).T
    for h in range(HEADS):
        cols = slice(h * HS, (h + 1) * HS)
        qt_v[h] = q_v[:, cols].T
        ogt_v[h] = og_v[:, cols].T
    pl.semaphore_wait(barrier, len(peers))
    for i in (2, 1, 3):
        px, device = x_peer(i)
        copy_to(tt_v.at[lax.rem(px, 2), mc], tx.at[mx, mc], fs_sem.at[2], fr_sem.at[2], device)
    for h in range(HEADS):
        f_w(h)
    wait_bytes(fr_sem.at[2], tx.at[pl.ds(0, NX - 1), 0])
    for i in (1, 2, 3):
        px = x_peer(i)[0]
        copy_to(tx.at[px, mc], tx.at[px, mc], fs_sem.at[3], fr_sem.at[3], core_peer)
    wait_bytes(fr_sem.at[3], tx.at[pl.ds(0, NX - 1), 0])
    for i in range(1, NX):
        px = x_peer(i)[0]
        txt[px] = tx[px].reshape(FEAT, TH).T
    f_y(0)
    f_y(1)
    f_y(2)
    f_ay(0)
    f_ay(1)
    f_ay(2)
    f_ax(0)
    f_ax(1)
    f_ax(2)
    attend(0)
    attend(1)
    attend(2)
    b_y(0)
    b_y(1)
    b_ay(0)
    b_y(2)
    b_ay(1)
    b_ax(0)
    b_ay(2)
    b_ax(1)
    finish(0)
    b_ax(2)
    finish(1)
    finish(2)

    wait_bytes(fr_sem.at[0], tc)
    ts[...] = (tp[:, mc] + tc[...]).astype(BF)
    for i in FAR_FIRST:
        pz, device = z_peer(i)
        copy_to(ts.at[pz], tz.at[mz], fs_sem.at[1], fr_sem.at[1], device)
    for h in range(HEADS):
        for stage in range(8):
            wait(ssem, h, stage)
    wait_bytes(fs_sem.at[0], tc)
    wait_bytes(fs_sem.at[2], tx.at[pl.ds(0, NX - 1), 0])
    wait_bytes(fs_sem.at[3], tx.at[pl.ds(0, NX - 1), 0])
    wait_bytes(fr_sem.at[1], tz.at[pl.ds(0, NZ - 1)])
    t = tp[mz, mc] + tc[mz]
    for i in range(1, NZ):
        t = t + tz[z_peer(i)[0]].astype(F32)
    tg_ref[...] = t
    wait_bytes(fs_sem.at[1], tz.at[pl.ds(0, NZ - 1)])


def in_hbm(a):
    return pltpu.with_memory_space_constraint(a, pltpu.HBM)


def write_out(*refs):
    n = len(refs) // 2
    copies = [
        pltpu.make_async_copy(refs[i], refs[n + i], refs[-1].at[i]) for i in range(n)
    ]
    for copy in copies:
        copy.start()
    for copy in copies:
        copy.wait()


def local(queries, text, key_weight, value_weight, out_grad):
    width = HEADS * HS
    vm = pltpu.VMEM
    dma = pltpu.SemaphoreType.DMA
    held = pl.pallas_call(
        kernel,
        name="cross_attention",
        out_shape=(
            pltpu.VMEM((ROWS, width), BF),
            pltpu.VMEM((ROWS, width), BF),
            pltpu.VMEM((FEAT, width), F32),
            pltpu.VMEM((FEAT, width), F32),
            pltpu.VMEM((ZT, FEAT), F32),
        ),
        in_specs=[pl.BlockSpec(memory_space=pltpu.HBM)] * 5,
        out_specs=tuple([pl.BlockSpec(memory_space=pltpu.VMEM)] * 5),
        scratch_shapes=[
            vm((ROWS, width), BF), vm((ROWS, width), BF),
            vm((2, NC, FH, TH), BF), vm((2, HEADS, FEAT, HS), BF),
            vm((NX, NC, FH, TH), BF), vm((HEADS, NX, FEAT, HS), BF), vm((NX, TH, FEAT), BF),
            vm((HEADS, HS, ROWS), BF), vm((HEADS, HS, ROWS), BF),
            vm((HEADS, NY, YT, HS), F32), vm((HEADS, NY, YT, HS), F32),
            vm((HEADS, NX, NY, YT, HS), BF),
            vm((HEADS, NX, NY, YT, HS), BF), vm((HEADS, NX, NY, YT, HS), BF),
            vm((HEADS, NY, YT, HS), BF), vm((HEADS, NY, YT, HS), BF),
            vm((HEADS, NX, NY, YT, HS), BF),
            vm((NZ, NC, ZT, FEAT), F32), vm((NZ, ZT, FEAT), F32),
            vm((NZ, ZT, FEAT), BF), vm((NZ, ZT, FEAT), BF),
            dma((12,)), dma((HEADS, 8)), dma((HEADS, 8)), dma((4,)), dma((4,)),
        ],
        compiler_params=pltpu.CompilerParams(
            collective_id=0, has_side_effects=True, vmem_limit_bytes=48 * 1024 * 1024
        ),
    )(*(in_hbm(a) for a in (queries, text.T, key_weight, value_weight, out_grad)))
    return pl.pallas_call(
        write_out,
        name="write_out",
        out_shape=tuple(jax.ShapeDtypeStruct(a.shape, a.dtype) for a in held),
        in_specs=[pl.BlockSpec(memory_space=pltpu.VMEM)] * 5,
        out_specs=tuple([pl.BlockSpec(memory_space=pl.ANY)] * 5),
        scratch_shapes=[dma((5,))],
        compiler_params=pltpu.CompilerParams(vmem_limit_bytes=1024 * 1024),
    )(*held)


def solution(mesh):
    in_specs = (
        P("seq", "head"),
        P(None, "seq"),
        P("seq", "head"),
        P("seq", "head"),
        P("seq", "head"),
    )
    out_specs = (
        P("seq", "head"),
        P("seq", "head"),
        P("seq", "head"),
        P("seq", "head"),
        P("head", "seq"),
    )
    return jax.shard_map(local, mesh=mesh, in_specs=in_specs, out_specs=out_specs, check_vma=False)
```

```python
import jax
import jax.numpy as jnp
from jax import lax
from jax.experimental import pallas as pl
from jax.experimental.pallas import tpu as pltpu
from jax.sharding import PartitionSpec as P

MESH = pl.DeviceIdType.MESH
NX, NY, NZ, NC = 4, 8, 8, 2
HS = 128
HEADS = 3
TEXT = 512
FEAT = 192
WIDE = 256
ROWS = 1024
TH = TEXT // 2
YT = TH // NY
FH = FEAT // 2
ZT = TEXT // (NZ * NC)
SCALE = 1.0 / HS**0.5
EXP2_SCALE = SCALE * 1.4426950408889634
BF = jnp.bfloat16
F32 = jnp.float32

S_W, S_Y, S_AY, S_AX, S_GX, S_GY, S_GAY, S_GAX = range(8)
FAR_FIRST = (4, 3, 5, 2, 6, 1, 7)


def head_cols(h):
    return pl.ds(pl.multiple_of(h * HS, HS), HS)


def each(count, step):
    def body(i, carry):
        step(i)
        return carry

    lax.fori_loop(0, count, body, 0)


def dot(a, b):
    return jnp.dot(a, b, preferred_element_type=F32)


def kernel(
    q_hbm, tt_hbm, kw_hbm, vw_hbm, og_hbm,
    o_ref, dq_ref, kwg_ref, vwg_ref, tg_ref,
    q_v, og_v, tt_v, w_v, tx, wx, txt, qt_v, ogt_v,
    ks, ky, kvf, gp, gx, gs, gy, gf,
    tp, tc, ts, tz,
    in_sem, ssem, rsem, fs_sem, fr_sem,
):
    seq = lax.axis_index("seq")
    head = lax.axis_index("head")
    mx, my = seq // NY, lax.rem(seq, NY)
    mz, mc = head // NC, lax.rem(head, NC)
    mb, ma = mx // 2, lax.rem(mx, 2)

    def x_peer(i):
        px = lax.rem(mx + i, NX)
        return px, (px * NY + my, head)

    def y_peer(i):
        py = lax.rem(my + i, NY)
        return py, (mx * NY + py, head)

    def z_peer(i):
        pz = lax.rem(mz + i, NZ)
        return pz, (seq, pz * NC + mc)

    core_peer = (seq, mz * NC + (1 - mc))

    barrier = pltpu.get_barrier_semaphore()
    peers = [x_peer(i)[1] for i in range(1, NX)] + [y_peer(i)[1] for i in range(1, NY)]
    peers += [z_peer(i)[1] for i in range(1, NZ)] + [core_peer]
    for peer in peers:
        pl.semaphore_signal(barrier, inc=1, device_id=peer, device_id_type=MESH)

    loads = []
    for a in range(2):
        for c in range(NC):
            loads.append((tt_hbm.at[pl.ds(c * FH, FH), pl.ds(a * TH, TH)], tt_v.at[a, c]))
    for h in range(HEADS):
        loads.append((kw_hbm.at[:, pl.ds(h * HS, HS)], w_v.at[0, h]))
        loads.append((vw_hbm.at[:, pl.ds(h * HS, HS)], w_v.at[1, h]))
    loads += [(q_hbm, q_v), (og_hbm, og_v)]
    loads = [pltpu.make_async_copy(a, b, in_sem.at[i]) for i, (a, b) in enumerate(loads)]
    for load in loads:
        load.start()

    def copy_to(src, dst, s_sem, r_sem, device):
        pltpu.make_async_remote_copy(
            src_ref=src, dst_ref=dst, send_sem=s_sem, recv_sem=r_sem,
            device_id=device, device_id_type=MESH,
        ).start()

    def send(src, dst, h, stage, device):
        copy_to(src, dst, ssem.at[h, stage], rsem.at[h, stage], device)

    def wait_bytes(sem, ref):
        pltpu.make_async_copy(ref, ref, sem).wait()

    def wait(sem, h, stage):
        ref = {
            S_W: wx.at[h, pl.ds(0, NX - 1)],
            S_Y: ky.at[h, pl.ds(0, NY - 1)],
            S_AY: kvf.at[h, 0, pl.ds(0, NY - 1)],
            S_AX: kvf.at[h, pl.ds(0, NX - 1)],
            S_GX: gx.at[h, pl.ds(0, NX - 1)],
            S_GY: gy.at[h, pl.ds(0, NY - 1)],
            S_GAY: gf.at[h, 0, pl.ds(0, NY - 1)],
            S_GAX: gf.at[h, pl.ds(0, NX - 1)],
        }[stage]
        wait_bytes(sem.at[h, stage], ref)

    def spread_y(full, h, stage):
        for i in FAR_FIRST:
            send(full.at[h, mx, my], full.at[h, mx, my], h, stage, y_peer(i)[1])

    def spread_x(full, h, before, stage):
        wait(rsem, h, before)
        for i in (2, 1, 3):
            send(full.at[h, mx], full.at[h, mx], h, stage, x_peer(i)[1])

    def f_w(h):
        for i in (2, 1, 3):
            px, device = x_peer(i)
            send(w_v.at[px // 2, h], wx.at[h, mx], h, S_W, device)

    def f_y(h):
        wait(rsem, h, S_W)
        p = dot(txt[mx], w_v[mb, h])
        for i in range(1, NX):
            px = x_peer(i)[0]
            p = p + dot(txt[px], wx[h, px])
        ks[h] = p.reshape(NY, YT, HS)
        for i in FAR_FIRST:
            py, device = y_peer(i)
            send(ks.at[h, py], ky.at[h, my], h, S_Y, device)

    def f_ay(h):
        wait(rsem, h, S_Y)
        k = ks[h, my]
        for i in range(1, NY):
            k = k + ky[h, y_peer(i)[0]]
        kvf[h, mx, my] = k.astype(BF)
        spread_y(kvf, h, S_AY)

    def f_ax(h):
        spread_x(kvf, h, S_AY, S_AX)

    def attend(h):
        wait(rsem, h, S_AX)
        cols = head_cols(h)
        k = kvf[h, 0:2].reshape(TEXT, HS)
        v = kvf[h, 2:4].reshape(TEXT, HS)
        s = dot(k, qt_v[h])
        e = jnp.exp2((s - jnp.max(s, axis=0, keepdims=True)) * EXP2_SCALE)
        p = e * (1.0 / jnp.sum(e, axis=0, keepdims=True))
        low = p.astype(BF)
        gp[h, 2:4] = dot(low, og_v[:, cols]).astype(BF).reshape(2, NY, YT, HS)
        dp = dot(v, ogt_v[h])
        delta = jnp.sum(p * dp, axis=0, keepdims=True)
        ds = (p * (dp - delta) * SCALE).astype(BF)
        gp[h, 0:2] = dot(ds, q_v[:, cols]).astype(BF).reshape(2, NY, YT, HS)
        for i in (2, 1, 3):
            px, device = x_peer(i)
            send(gp.at[h, px], gx.at[h, mx], h, S_GX, device)
        o_ref[:, cols] = dot(v.T, low).T.astype(BF)
        dq_ref[:, cols] = dot(k.T, ds).T.astype(BF)

    def b_y(h):
        wait(rsem, h, S_GX)
        g = gp[h, mx].astype(F32)
        for i in range(1, NX):
            g = g + gx[h, x_peer(i)[0]].astype(F32)
        gs[h] = g.astype(BF)
        for i in FAR_FIRST:
            py, device = y_peer(i)
            send(gs.at[h, py], gy.at[h, my], h, S_GY, device)

    def b_ay(h):
        wait(rsem, h, S_GY)
        g = gs[h, my].astype(F32)
        for i in range(1, NY):
            g = g + gy[h, y_peer(i)[0]].astype(F32)
        gf[h, mx, my] = g.astype(BF)
        spread_y(gf, h, S_GAY)

    def b_ax(h):
        spread_x(gf, h, S_GAY, S_GAX)

    def finish(h):
        wait(rsem, h, S_GAX)
        cols = head_cols(h)
        part = 0.0
        for j in range(2):
            g = gf[h, 2 * j : 2 * j + 2].reshape(TEXT, HS)
            part = part + lax.dot_general(
                g, w_v[j, h], (((1,), (1,)), ((), ())), preferred_element_type=F32
            )
        tp[:, :, :, :FEAT] += part.reshape(NZ, NC, ZT, FEAT)

        @pl.when(h == HEADS - 1)
        def _():
            copy_to(tp.at[:, 1 - mc], tc, fs_sem.at[0], fr_sem.at[0], core_peer)

        for j, ref in enumerate((kwg_ref, vwg_ref)):
            wg = 0.0
            for a in range(2):
                wg = wg + dot(tt_v[a].reshape(FEAT, TH), gf[h, 2 * j + a].reshape(TH, HS))
            ref[:, cols] = wg

    tp[...] = jnp.zeros_like(tp)
    for load in loads:
        load.wait()
    txt[mx] = tt_v[ma].reshape(FEAT, TH).T

    def turn(h):
        cols = head_cols(h)
        qt_v[h] = q_v[:, cols].T
        ogt_v[h] = og_v[:, cols].T

    pl.when(mc == 0)(lambda: each(HEADS, turn))
    pl.semaphore_wait(barrier, len(peers))
    for i in (2, 1, 3):
        px, device = x_peer(i)
        copy_to(tt_v.at[lax.rem(px, 2), mc], tx.at[mx, mc], fs_sem.at[2], fr_sem.at[2], device)
    pl.when(mc == 0)(lambda: each(HEADS, f_w))
    wait_bytes(fr_sem.at[2], tx.at[pl.ds(0, NX - 1), 0])
    for i in (1, 2, 3):
        px = x_peer(i)[0]
        copy_to(tx.at[px, mc], tx.at[px, mc], fs_sem.at[3], fr_sem.at[3], core_peer)
    wait_bytes(fr_sem.at[3], tx.at[pl.ds(0, NX - 1), 0])
    for i in range(1, NX):
        px = x_peer(i)[0]
        txt[px] = tx[px].reshape(FEAT, TH).T

    def gather(i):
        pl.when(i < HEADS)(lambda: f_ay(i))
        pl.when(i >= 1)(lambda: f_ax(i - 1))

    def grads(i):
        pl.when(i < HEADS)(lambda: b_y(i))
        pl.when((i >= 1) & (i <= HEADS))(lambda: b_ay(i - 1))
        pl.when(i >= 2)(lambda: b_ax(i - 2))

    @pl.when(mc == 1)
    def _():
        each(HEADS, turn)
        each(HEADS, f_w)

    each(HEADS, f_y)
    each(HEADS + 1, gather)
    each(HEADS, attend)
    each(HEADS + 2, grads)
    each(HEADS, finish)

    wait_bytes(fr_sem.at[0], tc)
    ts[...] = (tp[:, mc] + tc[...]).astype(BF)
    for i in FAR_FIRST:
        pz, device = z_peer(i)
        copy_to(ts.at[pz], tz.at[mz], fs_sem.at[1], fr_sem.at[1], device)

    def sent(h):
        for stage in range(8):
            wait(ssem, h, stage)

    each(HEADS, sent)
    wait_bytes(fs_sem.at[0], tc)
    wait_bytes(fs_sem.at[2], tx.at[pl.ds(0, NX - 1), 0])
    wait_bytes(fs_sem.at[3], tx.at[pl.ds(0, NX - 1), 0])
    wait_bytes(fr_sem.at[1], tz.at[pl.ds(0, NZ - 1)])
    t = tp[mz, mc] + tc[mz]
    for i in range(1, NZ):
        t = t + tz[z_peer(i)[0]].astype(F32)
    tg_ref[...] = t[:, :FEAT]
    wait_bytes(fs_sem.at[1], tz.at[pl.ds(0, NZ - 1)])


def in_hbm(a):
    return pltpu.with_memory_space_constraint(a, pltpu.HBM)


def write_out(*refs):
    n = len(refs) // 2
    copies = [
        pltpu.make_async_copy(refs[i], refs[n + i], refs[-1].at[i]) for i in range(n)
    ]
    for copy in copies:
        copy.start()
    for copy in copies:
        copy.wait()


def local(queries, text, key_weight, value_weight, out_grad):
    width = HEADS * HS
    vm = pltpu.VMEM
    dma = pltpu.SemaphoreType.DMA
    held = pl.pallas_call(
        kernel,
        name="cross_attention",
        out_shape=(
            pltpu.VMEM((ROWS, width), BF),
            pltpu.VMEM((ROWS, width), BF),
            pltpu.VMEM((FEAT, width), F32),
            pltpu.VMEM((FEAT, width), F32),
            pltpu.VMEM((ZT, FEAT), F32),
        ),
        in_specs=[pl.BlockSpec(memory_space=pltpu.HBM)] * 5,
        out_specs=tuple([pl.BlockSpec(memory_space=pltpu.VMEM)] * 5),
        scratch_shapes=[
            vm((ROWS, width), BF), vm((ROWS, width), BF),
            vm((2, NC, FH, TH), BF), vm((2, HEADS, FEAT, HS), BF),
            vm((NX, NC, FH, TH), BF), vm((HEADS, NX, FEAT, HS), BF), vm((NX, TH, FEAT), BF),
            vm((HEADS, HS, ROWS), BF), vm((HEADS, HS, ROWS), BF),
            vm((HEADS, NY, YT, HS), F32), vm((HEADS, NY, YT, HS), F32),
            vm((HEADS, NX, NY, YT, HS), BF),
            vm((HEADS, NX, NY, YT, HS), BF), vm((HEADS, NX, NY, YT, HS), BF),
            vm((HEADS, NY, YT, HS), BF), vm((HEADS, NY, YT, HS), BF),
            vm((HEADS, NX, NY, YT, HS), BF),
            vm((NZ, NC, ZT, WIDE), F32), vm((NZ, ZT, WIDE), F32),
            vm((NZ, ZT, WIDE), BF), vm((NZ, ZT, WIDE), BF),
            dma((12,)), dma((HEADS, 8)), dma((HEADS, 8)), dma((4,)), dma((4,)),
        ],
        compiler_params=pltpu.CompilerParams(
            collective_id=0, has_side_effects=True, vmem_limit_bytes=48 * 1024 * 1024
        ),
    )(*(in_hbm(a) for a in (queries, text.T, key_weight, value_weight, out_grad)))
    return pl.pallas_call(
        write_out,
        name="write_out",
        out_shape=tuple(jax.ShapeDtypeStruct(a.shape, a.dtype) for a in held),
        in_specs=[pl.BlockSpec(memory_space=pltpu.VMEM)] * 5,
        out_specs=tuple([pl.BlockSpec(memory_space=pl.ANY)] * 5),
        scratch_shapes=[dma((5,))],
        compiler_params=pltpu.CompilerParams(vmem_limit_bytes=1024 * 1024),
    )(*held)


def solution(mesh):
    in_specs = (
        P("seq", "head"),
        P(None, "seq"),
        P("seq", "head"),
        P("seq", "head"),
        P("seq", "head"),
    )
    out_specs = (
        P("seq", "head"),
        P("seq", "head"),
        P("seq", "head"),
        P("seq", "head"),
        P("head", "seq"),
    )
    return jax.shard_map(local, mesh=mesh, in_specs=in_specs, out_specs=out_specs, check_vma=False)
```

```python
import jax
import jax.numpy as jnp
from jax import lax
from jax.experimental import pallas as pl
from jax.experimental.pallas import tpu as pltpu
from jax.sharding import PartitionSpec as P

MESH = pl.DeviceIdType.MESH
NX, NY, NZ, NC = 4, 8, 8, 2
HS = 128
HEADS = 3
TEXT = 512
FEAT = 192
WIDE = 256
ROWS = 1024
TH = TEXT // 2
YT = TH // NY
FH = FEAT // 2
ZT = TEXT // (NZ * NC)
SCALE = 1.0 / HS**0.5
EXP2_SCALE = SCALE * 1.4426950408889634
BF = jnp.bfloat16
F32 = jnp.float32

S_W, S_Y, S_AY, S_AX, S_GX, S_GY, S_GAY, S_GAX = range(8)
FAR_FIRST = (4, 3, 5, 2, 6, 1, 7)


def head_cols(h):
    return pl.ds(pl.multiple_of(h * HS, HS), HS)


def each(count, step):
    def body(i, carry):
        step(i)
        return carry

    lax.fori_loop(0, count, body, 0)


def dot(a, b):
    return jnp.dot(a, b, preferred_element_type=F32)


def kernel(
    q_hbm, tt_hbm, kw_hbm, vw_hbm, og_hbm,
    o_ref, dq_ref, kwg_ref, vwg_ref, tg_ref,
    q_v, og_v, tt_v, w_v, tx, wx, txt, qt_v, ogt_v,
    ks, ky, kvf, gp, gx, gs, gy, gf,
    tp, tc, ts, tz,
    in_sem, ssem, rsem, fs_sem, fr_sem,
):
    seq = lax.axis_index("seq")
    head = lax.axis_index("head")
    mx, my = seq // NY, lax.rem(seq, NY)
    mz, mc = head // NC, lax.rem(head, NC)
    mb, ma = mx // 2, lax.rem(mx, 2)

    def x_peer(i):
        px = lax.rem(mx + i, NX)
        return px, (px * NY + my, head)

    def y_peer(i):
        py = lax.rem(my + i, NY)
        return py, (mx * NY + py, head)

    def z_peer(i):
        pz = lax.rem(mz + i, NZ)
        return pz, (seq, pz * NC + mc)

    core_peer = (seq, mz * NC + (1 - mc))

    barrier = pltpu.get_barrier_semaphore()
    peers = [x_peer(i)[1] for i in range(1, NX)] + [y_peer(i)[1] for i in range(1, NY)]
    peers += [z_peer(i)[1] for i in range(1, NZ)] + [core_peer]
    for peer in peers:
        pl.semaphore_signal(barrier, inc=1, device_id=peer, device_id_type=MESH)

    loads = []
    for a in range(2):
        for c in range(NC):
            loads.append((tt_hbm.at[pl.ds(c * FH, FH), pl.ds(a * TH, TH)], tt_v.at[a, c]))
    for h in range(HEADS):
        loads.append((kw_hbm.at[:, pl.ds(h * HS, HS)], w_v.at[0, h]))
        loads.append((vw_hbm.at[:, pl.ds(h * HS, HS)], w_v.at[1, h]))
    loads += [(q_hbm, q_v), (og_hbm, og_v)]
    loads = [pltpu.make_async_copy(a, b, in_sem.at[i]) for i, (a, b) in enumerate(loads)]
    for load in loads:
        load.start()

    def copy_to(src, dst, s_sem, r_sem, device):
        pltpu.make_async_remote_copy(
            src_ref=src, dst_ref=dst, send_sem=s_sem, recv_sem=r_sem,
            device_id=device, device_id_type=MESH,
        ).start()

    def send(src, dst, h, stage, device):
        copy_to(src, dst, ssem.at[h, stage], rsem.at[h, stage], device)

    def wait_bytes(sem, ref):
        pltpu.make_async_copy(ref, ref, sem).wait()

    def wait(sem, h, stage):
        ref = {
            S_W: wx.at[h, pl.ds(0, NX - 1)],
            S_Y: ky.at[h, pl.ds(0, NY - 1)],
            S_AY: kvf.at[h, 0, pl.ds(0, NY - 1)],
            S_AX: kvf.at[h, pl.ds(0, NX - 1)],
            S_GX: gx.at[h, pl.ds(0, NX - 1)],
            S_GY: gy.at[h, pl.ds(0, NY - 1)],
            S_GAY: gf.at[h, 0, pl.ds(0, NY - 1)],
            S_GAX: gf.at[h, pl.ds(0, NX - 1)],
        }[stage]
        wait_bytes(sem.at[h, stage], ref)

    def spread_y(full, h, stage):
        for i in FAR_FIRST:
            send(full.at[h, mx, my], full.at[h, mx, my], h, stage, y_peer(i)[1])

    def spread_x(full, h, before, stage):
        wait(rsem, h, before)
        for i in (2, 1, 3):
            send(full.at[h, mx], full.at[h, mx], h, stage, x_peer(i)[1])

    def f_w(h):
        for i in (2, 1, 3):
            px, device = x_peer(i)
            send(w_v.at[px // 2, h], wx.at[h, mx], h, S_W, device)

    def f_y(h):
        wait(rsem, h, S_W)
        p = dot(txt[mx], w_v[mb, h])
        for i in range(1, NX):
            px = x_peer(i)[0]
            p = p + dot(txt[px], wx[h, px])
        ks[h] = p.reshape(NY, YT, HS)
        for i in FAR_FIRST:
            py, device = y_peer(i)
            send(ks.at[h, py], ky.at[h, my], h, S_Y, device)

    def f_ay(h):
        wait(rsem, h, S_Y)
        k = ks[h, my]
        for i in range(1, NY):
            k = k + ky[h, y_peer(i)[0]]
        kvf[h, mx, my] = k.astype(BF)
        spread_y(kvf, h, S_AY)

    def f_ax(h):
        spread_x(kvf, h, S_AY, S_AX)

    def attend(h):
        wait(rsem, h, S_AX)
        cols = head_cols(h)
        k = kvf[h, 0:2].reshape(TEXT, HS)
        v = kvf[h, 2:4].reshape(TEXT, HS)
        s = dot(k, qt_v[h])
        e = jnp.exp2((s - jnp.max(s, axis=0, keepdims=True)) * EXP2_SCALE)
        p = e * (1.0 / jnp.sum(e, axis=0, keepdims=True))
        low = p.astype(BF)
        gp[h, 2:4] = dot(low, og_v[:, cols]).astype(BF).reshape(2, NY, YT, HS)
        dp = dot(v, ogt_v[h])
        delta = jnp.sum(p * dp, axis=0, keepdims=True)
        ds = (p * (dp - delta) * SCALE).astype(BF)
        gp[h, 0:2] = dot(ds, q_v[:, cols]).astype(BF).reshape(2, NY, YT, HS)
        for i in (2, 1, 3):
            px, device = x_peer(i)
            send(gp.at[h, px], gx.at[h, mx], h, S_GX, device)
        o_ref[:, cols] = dot(v.T, low).T.astype(BF)
        dq_ref[:, cols] = dot(k.T, ds).T.astype(BF)

    def b_y(h):
        wait(rsem, h, S_GX)
        g = gp[h, mx].astype(F32)
        for i in range(1, NX):
            g = g + gx[h, x_peer(i)[0]].astype(F32)
        gs[h] = g.astype(BF)
        for i in FAR_FIRST:
            py, device = y_peer(i)
            send(gs.at[h, py], gy.at[h, my], h, S_GY, device)

    def b_ay(h):
        wait(rsem, h, S_GY)
        g = gs[h, my].astype(F32)
        for i in range(1, NY):
            g = g + gy[h, y_peer(i)[0]].astype(F32)
        gf[h, mx, my] = g.astype(BF)
        spread_y(gf, h, S_GAY)

    def b_ax(h):
        spread_x(gf, h, S_GAY, S_GAX)

    def finish(h):
        wait(rsem, h, S_GAX)
        cols = head_cols(h)
        part = 0.0
        for j in range(2):
            g = gf[h, 2 * j : 2 * j + 2].reshape(TEXT, HS)
            part = part + lax.dot_general(
                g, w_v[j, h], (((1,), (1,)), ((), ())), preferred_element_type=F32
            )
        tp[:, :, :, :FEAT] += part.reshape(NZ, NC, ZT, FEAT)

        @pl.when(h == HEADS - 1)
        def _():
            copy_to(tp.at[:, 1 - mc], tc, fs_sem.at[0], fr_sem.at[0], core_peer)

        for j, ref in enumerate((kwg_ref, vwg_ref)):
            wg = 0.0
            for a in range(2):
                wg = wg + dot(tt_v[a].reshape(FEAT, TH), gf[h, 2 * j + a].reshape(TH, HS))
            ref[:, cols] = wg

    tp[...] = jnp.zeros_like(tp)
    for load in loads:
        load.wait()
    txt[mx] = tt_v[ma].reshape(FEAT, TH).T

    def turn(h):
        cols = head_cols(h)
        qt_v[h] = q_v[:, cols].T
        ogt_v[h] = og_v[:, cols].T

    pl.when(mc == 0)(lambda: each(HEADS, turn))
    pl.semaphore_wait(barrier, len(peers))
    for i in (2, 1, 3):
        px, device = x_peer(i)
        copy_to(tt_v.at[lax.rem(px, 2), mc], tx.at[mx, mc], fs_sem.at[2], fr_sem.at[2], device)
    pl.when(mc == 0)(lambda: each(HEADS, f_w))
    wait_bytes(fr_sem.at[2], tx.at[pl.ds(0, NX - 1), 0])
    for i in (1, 2, 3):
        px = x_peer(i)[0]
        copy_to(tx.at[px, mc], tx.at[px, mc], fs_sem.at[3], fr_sem.at[3], core_peer)
    wait_bytes(fr_sem.at[3], tx.at[pl.ds(0, NX - 1), 0])
    for i in range(1, NX):
        px = x_peer(i)[0]
        txt[px] = tx[px].reshape(FEAT, TH).T

    def gather(i):
        pl.when(i < HEADS)(lambda: f_ay(i))
        pl.when(i >= 1)(lambda: f_ax(i - 1))

    def grads(i):
        pl.when(i < HEADS)(lambda: b_y(i))
        pl.when((i >= 1) & (i <= HEADS))(lambda: b_ay(i - 1))
        pl.when(i >= 2)(lambda: b_ax(i - 2))

    def weights_and_sums(h):
        pl.when(mc == 1)(lambda: f_w(h))
        f_y(h)

    pl.when(mc == 1)(lambda: each(HEADS, turn))
    each(HEADS, weights_and_sums)
    each(HEADS + 1, gather)
    each(HEADS, attend)
    each(HEADS + 2, grads)
    each(HEADS, finish)

    wait_bytes(fr_sem.at[0], tc)
    ts[...] = (tp[:, mc] + tc[...]).astype(BF)
    for i in FAR_FIRST:
        pz, device = z_peer(i)
        copy_to(ts.at[pz], tz.at[mz], fs_sem.at[1], fr_sem.at[1], device)

    def sent(h):
        for stage in range(8):
            wait(ssem, h, stage)

    each(HEADS, sent)
    wait_bytes(fs_sem.at[0], tc)
    wait_bytes(fs_sem.at[2], tx.at[pl.ds(0, NX - 1), 0])
    wait_bytes(fs_sem.at[3], tx.at[pl.ds(0, NX - 1), 0])
    wait_bytes(fr_sem.at[1], tz.at[pl.ds(0, NZ - 1)])
    t = tp[mz, mc] + tc[mz]
    for i in range(1, NZ):
        t = t + tz[z_peer(i)[0]].astype(F32)
    tg_ref[...] = t[:, :FEAT]
    wait_bytes(fs_sem.at[1], tz.at[pl.ds(0, NZ - 1)])


def in_hbm(a):
    return pltpu.with_memory_space_constraint(a, pltpu.HBM)


def write_out(*refs):
    n = len(refs) // 2
    copies = [
        pltpu.make_async_copy(refs[i], refs[n + i], refs[-1].at[i]) for i in range(n)
    ]
    for copy in copies:
        copy.start()
    for copy in copies:
        copy.wait()


def local(queries, text, key_weight, value_weight, out_grad):
    width = HEADS * HS
    vm = pltpu.VMEM
    dma = pltpu.SemaphoreType.DMA
    held = pl.pallas_call(
        kernel,
        name="cross_attention",
        out_shape=(
            pltpu.VMEM((ROWS, width), BF),
            pltpu.VMEM((ROWS, width), BF),
            pltpu.VMEM((FEAT, width), F32),
            pltpu.VMEM((FEAT, width), F32),
            pltpu.VMEM((ZT, FEAT), F32),
        ),
        in_specs=[pl.BlockSpec(memory_space=pltpu.HBM)] * 5,
        out_specs=tuple([pl.BlockSpec(memory_space=pltpu.VMEM)] * 5),
        scratch_shapes=[
            vm((ROWS, width), BF), vm((ROWS, width), BF),
            vm((2, NC, FH, TH), BF), vm((2, HEADS, FEAT, HS), BF),
            vm((NX, NC, FH, TH), BF), vm((HEADS, NX, FEAT, HS), BF), vm((NX, TH, FEAT), BF),
            vm((HEADS, HS, ROWS), BF), vm((HEADS, HS, ROWS), BF),
            vm((HEADS, NY, YT, HS), F32), vm((HEADS, NY, YT, HS), F32),
            vm((HEADS, NX, NY, YT, HS), BF),
            vm((HEADS, NX, NY, YT, HS), BF), vm((HEADS, NX, NY, YT, HS), BF),
            vm((HEADS, NY, YT, HS), BF), vm((HEADS, NY, YT, HS), BF),
            vm((HEADS, NX, NY, YT, HS), BF),
            vm((NZ, NC, ZT, WIDE), F32), vm((NZ, ZT, WIDE), F32),
            vm((NZ, ZT, WIDE), BF), vm((NZ, ZT, WIDE), BF),
            dma((12,)), dma((HEADS, 8)), dma((HEADS, 8)), dma((4,)), dma((4,)),
        ],
        compiler_params=pltpu.CompilerParams(
            collective_id=0, has_side_effects=True, vmem_limit_bytes=48 * 1024 * 1024
        ),
    )(*(in_hbm(a) for a in (queries, text.T, key_weight, value_weight, out_grad)))
    return pl.pallas_call(
        write_out,
        name="write_out",
        out_shape=tuple(jax.ShapeDtypeStruct(a.shape, a.dtype) for a in held),
        in_specs=[pl.BlockSpec(memory_space=pltpu.VMEM)] * 5,
        out_specs=tuple([pl.BlockSpec(memory_space=pl.ANY)] * 5),
        scratch_shapes=[dma((5,))],
        compiler_params=pltpu.CompilerParams(vmem_limit_bytes=1024 * 1024),
    )(*held)


def solution(mesh):
    in_specs = (
        P("seq", "head"),
        P(None, "seq"),
        P("seq", "head"),
        P("seq", "head"),
        P("seq", "head"),
    )
    out_specs = (
        P("seq", "head"),
        P("seq", "head"),
        P("seq", "head"),
        P("seq", "head"),
        P("head", "seq"),
    )
    return jax.shard_map(local, mesh=mesh, in_specs=in_specs, out_specs=out_specs, check_vma=False)
```

```python
import jax
import jax.numpy as jnp
from jax import lax
from jax.experimental import pallas as pl
from jax.experimental.pallas import tpu as pltpu
from jax.sharding import PartitionSpec as P

MESH = pl.DeviceIdType.MESH
NX, NY, NZ, NC = 4, 8, 8, 2
HS = 128
HEADS = 3
TEXT = 512
FEAT = 192
WIDE = 256
ROWS = 1024
TH = TEXT // 2
YT = TH // NY
FH = FEAT // 2
ZT = TEXT // (NZ * NC)
SCALE = 1.0 / HS**0.5
EXP2_SCALE = SCALE * 1.4426950408889634
BF = jnp.bfloat16
F32 = jnp.float32

S_W, S_Y, S_AY, S_AX, S_GX, S_GY, S_GAY, S_GAX = range(8)
FAR_FIRST = (4, 3, 5, 2, 6, 1, 7)


def head_cols(h):
    return pl.ds(pl.multiple_of(h * HS, HS), HS)


def each(count, step):
    def body(i, carry):
        step(i)
        return carry

    lax.fori_loop(0, count, body, 0)


def dot(a, b):
    return jnp.dot(a, b, preferred_element_type=F32)


def kernel(
    q_hbm, tt_hbm, kw_hbm, vw_hbm, og_hbm,
    o_ref, dq_ref, kwg_ref, vwg_ref, tg_ref,
    q_v, og_v, tt_v, w_v, tx, wx, txt, qt_v, ogt_v,
    ks, ky, kvf, gp, gx, gs, gy, gf,
    tp, tc, ts, tz,
    in_sem, ssem, rsem, fs_sem, fr_sem,
):
    seq = lax.axis_index("seq")
    head = lax.axis_index("head")
    mx, my = seq // NY, lax.rem(seq, NY)
    mz, mc = head // NC, lax.rem(head, NC)
    mb, ma = mx // 2, lax.rem(mx, 2)

    def x_peer(i):
        px = lax.rem(mx + i, NX)
        return px, (px * NY + my, head)

    def y_peer(i):
        py = lax.rem(my + i, NY)
        return py, (mx * NY + py, head)

    def z_peer(i):
        pz = lax.rem(mz + i, NZ)
        return pz, (seq, pz * NC + mc)

    core_peer = (seq, mz * NC + (1 - mc))

    barrier = pltpu.get_barrier_semaphore()
    peers = [x_peer(i)[1] for i in range(1, NX)] + [y_peer(i)[1] for i in range(1, NY)]
    peers += [z_peer(i)[1] for i in range(1, NZ)] + [core_peer]
    for peer in peers:
        pl.semaphore_signal(barrier, inc=1, device_id=peer, device_id_type=MESH)

    loads = []
    for a in range(2):
        for c in range(NC):
            loads.append((tt_hbm.at[pl.ds(c * FH, FH), pl.ds(a * TH, TH)], tt_v.at[a, c]))
    for h in range(HEADS):
        loads.append((kw_hbm.at[:, pl.ds(h * HS, HS)], w_v.at[0, h]))
        loads.append((vw_hbm.at[:, pl.ds(h * HS, HS)], w_v.at[1, h]))
    loads += [(q_hbm, q_v), (og_hbm, og_v)]
    loads = [pltpu.make_async_copy(a, b, in_sem.at[i]) for i, (a, b) in enumerate(loads)]
    for load in loads:
        load.start()

    def copy_to(src, dst, s_sem, r_sem, device):
        pltpu.make_async_remote_copy(
            src_ref=src, dst_ref=dst, send_sem=s_sem, recv_sem=r_sem,
            device_id=device, device_id_type=MESH,
        ).start()

    def send(src, dst, h, stage, device):
        copy_to(src, dst, ssem.at[h, stage], rsem.at[h, stage], device)

    def wait_bytes(sem, ref):
        pltpu.make_async_copy(ref, ref, sem).wait()

    def wait(sem, h, stage):
        ref = {
            S_W: wx.at[h, pl.ds(0, NX - 1)],
            S_Y: ky.at[h, pl.ds(0, NY - 1)],
            S_AY: kvf.at[h, 0, pl.ds(0, NY - 1)],
            S_AX: kvf.at[h, pl.ds(0, NX - 1)],
            S_GX: gx.at[h, pl.ds(0, NX - 1)],
            S_GY: gy.at[h, pl.ds(0, NY - 1)],
            S_GAY: gf.at[h, 0, pl.ds(0, NY - 1)],
            S_GAX: gf.at[h, pl.ds(0, NX - 1)],
        }[stage]
        wait_bytes(sem.at[h, stage], ref)

    def spread_y(full, h, stage):
        for i in FAR_FIRST:
            send(full.at[h, mx, my], full.at[h, mx, my], h, stage, y_peer(i)[1])

    def spread_x(full, h, before, stage):
        wait(rsem, h, before)
        for i in (2, 1, 3):
            send(full.at[h, mx], full.at[h, mx], h, stage, x_peer(i)[1])

    def f_w(h):
        for i in (2, 1, 3):
            px, device = x_peer(i)
            send(w_v.at[px // 2, h], wx.at[h, mx], h, S_W, device)

    def f_y(h):
        wait(rsem, h, S_W)
        p = dot(txt[mx], w_v[mb, h])
        for i in range(1, NX):
            px = x_peer(i)[0]
            p = p + dot(txt[px], wx[h, px])
        ks[h] = p.reshape(NY, YT, HS)
        for i in FAR_FIRST:
            py, device = y_peer(i)
            send(ks.at[h, py], ky.at[h, my], h, S_Y, device)

    def f_ay(h):
        wait(rsem, h, S_Y)
        k = ks[h, my]
        for i in range(1, NY):
            k = k + ky[h, y_peer(i)[0]]
        kvf[h, mx, my] = k.astype(BF)
        spread_y(kvf, h, S_AY)

    def f_ax(h):
        spread_x(kvf, h, S_AY, S_AX)

    def attend(h):
        wait(rsem, h, S_AX)
        cols = head_cols(h)
        k = kvf[h, 0:2].reshape(TEXT, HS)
        v = kvf[h, 2:4].reshape(TEXT, HS)
        s = dot(k, qt_v[h])
        e = jnp.exp2((s - jnp.max(s, axis=0, keepdims=True)) * EXP2_SCALE)
        p = e * (1.0 / jnp.sum(e, axis=0, keepdims=True))
        low = p.astype(BF)
        gp[h, 2:4] = dot(low, og_v[:, cols]).astype(BF).reshape(2, NY, YT, HS)
        dp = dot(v, ogt_v[h])
        delta = jnp.sum(p * dp, axis=0, keepdims=True)
        ds = (p * (dp - delta) * SCALE).astype(BF)
        gp[h, 0:2] = dot(ds, q_v[:, cols]).astype(BF).reshape(2, NY, YT, HS)

        def send_grads():
            for i in (2, 1, 3):
                px, device = x_peer(i)
                send(gp.at[h, px], gx.at[h, mx], h, S_GX, device)

        pl.when(mc == 0)(send_grads)
        o_ref[:, cols] = dot(v.T, low).T.astype(BF)
        dq_ref[:, cols] = dot(k.T, ds).T.astype(BF)
        pl.when(mc == 1)(send_grads)

    def b_y(h):
        wait(rsem, h, S_GX)
        g = gp[h, mx].astype(F32)
        for i in range(1, NX):
            g = g + gx[h, x_peer(i)[0]].astype(F32)
        gs[h] = g.astype(BF)
        for i in FAR_FIRST:
            py, device = y_peer(i)
            send(gs.at[h, py], gy.at[h, my], h, S_GY, device)

    def b_ay(h):
        wait(rsem, h, S_GY)
        g = gs[h, my].astype(F32)
        for i in range(1, NY):
            g = g + gy[h, y_peer(i)[0]].astype(F32)
        gf[h, mx, my] = g.astype(BF)
        spread_y(gf, h, S_GAY)

    def b_ax(h):
        spread_x(gf, h, S_GAY, S_GAX)

    def finish(h):
        wait(rsem, h, S_GAX)
        cols = head_cols(h)
        part = 0.0
        for j in range(2):
            g = gf[h, 2 * j : 2 * j + 2].reshape(TEXT, HS)
            part = part + lax.dot_general(
                g, w_v[j, h], (((1,), (1,)), ((), ())), preferred_element_type=F32
            )
        tp[:, :, :, :FEAT] += part.reshape(NZ, NC, ZT, FEAT)

        @pl.when(h == HEADS - 1)
        def _():
            copy_to(tp.at[:, 1 - mc], tc, fs_sem.at[0], fr_sem.at[0], core_peer)

        for j, ref in enumerate((kwg_ref, vwg_ref)):
            wg = 0.0
            for a in range(2):
                wg = wg + dot(tt_v[a].reshape(FEAT, TH), gf[h, 2 * j + a].reshape(TH, HS))
            ref[:, cols] = wg

    tp[...] = jnp.zeros_like(tp)
    for load in loads:
        load.wait()
    txt[mx] = tt_v[ma].reshape(FEAT, TH).T

    def turn(h):
        cols = head_cols(h)
        qt_v[h] = q_v[:, cols].T
        ogt_v[h] = og_v[:, cols].T

    pl.when(mc == 0)(lambda: each(HEADS, turn))
    pl.semaphore_wait(barrier, len(peers))
    for i in (2, 1, 3):
        px, device = x_peer(i)
        copy_to(tt_v.at[lax.rem(px, 2), mc], tx.at[mx, mc], fs_sem.at[2], fr_sem.at[2], device)
    pl.when(mc == 0)(lambda: each(HEADS, f_w))
    wait_bytes(fr_sem.at[2], tx.at[pl.ds(0, NX - 1), 0])
    for i in (1, 2, 3):
        px = x_peer(i)[0]
        copy_to(tx.at[px, mc], tx.at[px, mc], fs_sem.at[3], fr_sem.at[3], core_peer)
    wait_bytes(fr_sem.at[3], tx.at[pl.ds(0, NX - 1), 0])
    for i in range(1, NX):
        px = x_peer(i)[0]
        txt[px] = tx[px].reshape(FEAT, TH).T

    def gather(i):
        pl.when(i < HEADS)(lambda: f_ay(i))
        pl.when(i >= 1)(lambda: f_ax(i - 1))

    def grads(i):
        pl.when(i < HEADS)(lambda: b_y(i))
        pl.when((i >= 1) & (i <= HEADS))(lambda: b_ay(i - 1))
        pl.when(i >= 2)(lambda: b_ax(i - 2))

    def weights_and_sums(h):
        pl.when(mc == 1)(lambda: f_w(h))
        f_y(h)

    pl.when(mc == 1)(lambda: each(HEADS, turn))
    each(HEADS, weights_and_sums)
    each(HEADS + 1, gather)
    each(HEADS, attend)
    each(HEADS + 2, grads)
    each(HEADS, finish)

    wait_bytes(fr_sem.at[0], tc)
    ts[...] = (tp[:, mc] + tc[...]).astype(BF)
    for i in FAR_FIRST:
        pz, device = z_peer(i)
        copy_to(ts.at[pz], tz.at[mz], fs_sem.at[1], fr_sem.at[1], device)

    def sent(h):
        for stage in range(8):
            wait(ssem, h, stage)

    each(HEADS, sent)
    wait_bytes(fs_sem.at[0], tc)
    wait_bytes(fs_sem.at[2], tx.at[pl.ds(0, NX - 1), 0])
    wait_bytes(fs_sem.at[3], tx.at[pl.ds(0, NX - 1), 0])
    wait_bytes(fr_sem.at[1], tz.at[pl.ds(0, NZ - 1)])
    t = tp[mz, mc] + tc[mz]
    for i in range(1, NZ):
        t = t + tz[z_peer(i)[0]].astype(F32)
    tg_ref[...] = t[:, :FEAT]
    wait_bytes(fs_sem.at[1], tz.at[pl.ds(0, NZ - 1)])


def in_hbm(a):
    return pltpu.with_memory_space_constraint(a, pltpu.HBM)


def write_out(*refs):
    n = len(refs) // 2
    copies = [
        pltpu.make_async_copy(refs[i], refs[n + i], refs[-1].at[i]) for i in range(n)
    ]
    for copy in copies:
        copy.start()
    for copy in copies:
        copy.wait()


def local(queries, text, key_weight, value_weight, out_grad):
    width = HEADS * HS
    vm = pltpu.VMEM
    dma = pltpu.SemaphoreType.DMA
    held = pl.pallas_call(
        kernel,
        name="cross_attention",
        out_shape=(
            pltpu.VMEM((ROWS, width), BF),
            pltpu.VMEM((ROWS, width), BF),
            pltpu.VMEM((FEAT, width), F32),
            pltpu.VMEM((FEAT, width), F32),
            pltpu.VMEM((ZT, FEAT), F32),
        ),
        in_specs=[pl.BlockSpec(memory_space=pltpu.HBM)] * 5,
        out_specs=tuple([pl.BlockSpec(memory_space=pltpu.VMEM)] * 5),
        scratch_shapes=[
            vm((ROWS, width), BF), vm((ROWS, width), BF),
            vm((2, NC, FH, TH), BF), vm((2, HEADS, FEAT, HS), BF),
            vm((NX, NC, FH, TH), BF), vm((HEADS, NX, FEAT, HS), BF), vm((NX, TH, FEAT), BF),
            vm((HEADS, HS, ROWS), BF), vm((HEADS, HS, ROWS), BF),
            vm((HEADS, NY, YT, HS), F32), vm((HEADS, NY, YT, HS), F32),
            vm((HEADS, NX, NY, YT, HS), BF),
            vm((HEADS, NX, NY, YT, HS), BF), vm((HEADS, NX, NY, YT, HS), BF),
            vm((HEADS, NY, YT, HS), BF), vm((HEADS, NY, YT, HS), BF),
            vm((HEADS, NX, NY, YT, HS), BF),
            vm((NZ, NC, ZT, WIDE), F32), vm((NZ, ZT, WIDE), F32),
            vm((NZ, ZT, WIDE), BF), vm((NZ, ZT, WIDE), BF),
            dma((12,)), dma((HEADS, 8)), dma((HEADS, 8)), dma((4,)), dma((4,)),
        ],
        compiler_params=pltpu.CompilerParams(
            collective_id=0, has_side_effects=True, vmem_limit_bytes=48 * 1024 * 1024
        ),
    )(*(in_hbm(a) for a in (queries, text.T, key_weight, value_weight, out_grad)))
    return pl.pallas_call(
        write_out,
        name="write_out",
        out_shape=tuple(jax.ShapeDtypeStruct(a.shape, a.dtype) for a in held),
        in_specs=[pl.BlockSpec(memory_space=pltpu.VMEM)] * 5,
        out_specs=tuple([pl.BlockSpec(memory_space=pl.ANY)] * 5),
        scratch_shapes=[dma((5,))],
        compiler_params=pltpu.CompilerParams(vmem_limit_bytes=1024 * 1024),
    )(*held)


def solution(mesh):
    in_specs = (
        P("seq", "head"),
        P(None, "seq"),
        P("seq", "head"),
        P("seq", "head"),
        P("seq", "head"),
    )
    out_specs = (
        P("seq", "head"),
        P("seq", "head"),
        P("seq", "head"),
        P("seq", "head"),
        P("head", "seq"),
    )
    return jax.shard_map(local, mesh=mesh, in_specs=in_specs, out_specs=out_specs, check_vma=False)
```
